32 devices in a mesh: groups: 2 (over x), dp: 16 (over z, y, core).
Axes of the slice: x: 2, y: 2, z: 4, core: 2. Of those that a mesh axis runs over, the one named last changes fastest.
Arguments:
- tokens: bfloat16 [8192, 8192], P(('groups', 'dp')), parts along dimension 0, may hold values from -6 to 6
- out_grad: bfloat16 [8192, 512], P(('groups', 'dp')), parts along dimension 0, may hold values from -2.09375 to 2.09375
- base_weight: bfloat16 [8192, 512], P('dp'), may hold values from -0.0625 to 0.0625
- adapter_in: bfloat16 [8192, 4096], P('dp', 'groups'), parts along dimension 1, may hold values from -0.0625 to 0.0625
- adapter_out: bfloat16 [512, 4096], P('dp', 'groups'), parts along dimension 1, may hold values from -0.75 to 0.75
- tenant_ids: int32 [64], P('groups'), parts along dimension 0, may hold values from 0 to 31, as said below
Outputs:
- mixed: bfloat16 [8192, 512], P(('groups', 'dp')), parts along dimension 0
- layer_input_gradient: bfloat16 [8192, 8192], P(('groups', 'dp')), parts along dimension 0
- grad_in: bfloat16 [8192, 4096], P('dp', 'groups'), parts along dimension 1
- grad_out: bfloat16 [512, 4096], P('dp', 'groups'), parts along dimension 1
The draws below stay inside these ranges and needn't reach their ends.
There are 2 independent parts, one for each index of `groups`. The reference program is written for one: setup_inputs(seed, part) draws one part's arguments, and reference() takes and returns one part's arrays. A program takes and returns all parts, laid end to end along the dimension named above; an argument that names none is the same for every part. Nothing has to cross between parts.
Inputs may be any that keep to these rules, and one draw needn't show every extreme that they name: tenant_ids[s] names the adapter of window s; any adapter may be named by any number of windows, and the windows of one part may name up to 32 different adapters.
All inputs are finite; a program needn't handle non-finite values.
Results may differ from the reference program's by a relative error of at most 0.0049.
Values may be sent and summed in bfloat16 or wider, within the bound.
A program may use at most 128 MiB of HBM per device.

```python
import jax
import jax.numpy as jnp
from jax import lax

D = 8192
DOUT = 512
R = 64
TOK_SEQ = 128
SEQS = 32
TOKENS = 4096
ADAPTERS = 32


def draw_tenant_ids(key, part):
    key = jax.random.fold_in(key, 11)
    shuffle_key, position_key, choose_key = jax.random.split(key, 3)
    shuffled = jax.random.permutation(shuffle_key, jnp.arange(SEQS, dtype=jnp.int32) % ADAPTERS)
    position_order = jax.random.permutation(position_key, jnp.arange(SEQS, dtype=jnp.int32))
    chosen = jax.random.randint(choose_key, (SEQS,), 0, 4, dtype=jnp.int32)
    hot_ids = jnp.take(shuffled[:4], chosen)
    replaced = (position_order < SEQS // 4) & (shuffled != 0) & (shuffled != ADAPTERS - 1)
    return jnp.where(replaced, hot_ids, shuffled).astype(jnp.int32)


def steps_of(key, shape, pieces, low, largest):
    loudness, own = 1.0, jax.random.fold_in(key, 6)
    for dim, parts in pieces:
        heights = jnp.exp(jax.random.uniform(jax.random.fold_in(own, dim), (parts,), jnp.float32, low / len(pieces), largest / len(pieces)))
        loudness = loudness * jnp.repeat(heights, shape[dim] // parts).reshape([-1 if axis == dim else 1 for axis in range(len(shape))])
    return loudness


def centred(stream_key, extent, spread, limit, cuts=(), kind=jnp.bfloat16):
    drawn = spread * jax.random.normal(stream_key, extent, jnp.float32)
    if cuts:
        drawn = drawn * steps_of(stream_key, extent, cuts, -0.22, 0.18)
    return jnp.clip(drawn, -limit, limit).astype(kind)


def setup_inputs(seed: int = 0, part: int = 0) -> dict:
    arg_keys = jax.random.split(jax.random.key(seed), 7)
    part_keys = jax.random.split(jax.random.fold_in(arg_keys[6], part), 7)
    tokens = centred(part_keys[0], (TOKENS, D), 1.0, 6.0, ((0, 16),))
    out_grad = centred(part_keys[1], (TOKENS, DOUT), 0.35, 2.09375, ((0, 16),))
    base_weight = centred(arg_keys[2], (D, DOUT), D ** -0.5, 0.0625, ((0, 16),))
    adapter_in = centred(part_keys[3], (D, ADAPTERS * R), D ** -0.5, 0.0625, ((0, 16),))
    adapter_out = centred(part_keys[4], (DOUT, ADAPTERS * R), R ** -0.5, 0.75, ((0, 16),))
    tenant_ids = draw_tenant_ids(jax.random.fold_in(jax.random.fold_in(arg_keys[6], part), 71), part)
    return {"tokens": tokens, "out_grad": out_grad, "base_weight": base_weight, "adapter_in": adapter_in, "adapter_out": adapter_out, "tenant_ids": tenant_ids}


adapter_scale = 2.0


def reference(tokens, out_grad, base_weight, adapter_in, adapter_out, tenant_ids):
    seq_count = tenant_ids.shape[0]
    token_blocks = tokens.reshape(seq_count, TOK_SEQ, D)
    grad_blocks = out_grad.reshape(seq_count, TOK_SEQ, DOUT)
    in_table = adapter_in.reshape(D, ADAPTERS, R)
    out_table = adapter_out.reshape(DOUT, ADAPTERS, R)

    def per_window(items):
        block_x, gradient_block, tenant = items
        down_factor = lax.dynamic_index_in_dim(in_table, tenant.astype(jnp.int32), 1, keepdims=False)
        up_factor = lax.dynamic_index_in_dim(out_table, tenant.astype(jnp.int32), 1, keepdims=False)
        low_rank_product = jnp.dot(block_x, down_factor, preferred_element_type=jnp.float32).astype(jnp.bfloat16)
        adapter_output = jnp.dot(low_rank_product, up_factor.T, preferred_element_type=jnp.float32)
        frozen_output = jnp.dot(block_x, base_weight, preferred_element_type=jnp.float32)
        mixed = (frozen_output + adapter_scale * adapter_output).astype(jnp.bfloat16)
        gradient_low_rank = (adapter_scale * jnp.dot(gradient_block, up_factor, preferred_element_type=jnp.float32)).astype(jnp.bfloat16)
        frozen_input_gradient = jnp.dot(gradient_block, base_weight.T, preferred_element_type=jnp.float32)
        adapter_input_gradient = jnp.dot(gradient_low_rank, down_factor.T, preferred_element_type=jnp.float32)
        layer_input_gradient = (frozen_input_gradient + adapter_input_gradient).astype(jnp.bfloat16)
        term_in = jnp.dot(block_x.T, gradient_low_rank, preferred_element_type=jnp.float32)
        output_term = adapter_scale * jnp.dot(gradient_block.T, low_rank_product, preferred_element_type=jnp.float32)
        return mixed, layer_input_gradient, term_in, output_term

    mixed, layer_input_gradient, terms_in, terms_out = lax.map(per_window, (token_blocks, grad_blocks, tenant_ids))
    summed_in = jax.ops.segment_sum(terms_in, tenant_ids, num_segments=ADAPTERS)
    summed_out = jax.ops.segment_sum(terms_out, tenant_ids, num_segments=ADAPTERS)
    grad_in = jnp.transpose(summed_in, (1, 0, 2)).reshape(D, ADAPTERS * R).astype(jnp.bfloat16)
    grad_out = jnp.transpose(summed_out, (1, 0, 2)).reshape(DOUT, ADAPTERS * R).astype(jnp.bfloat16)
    return (mixed.reshape(seq_count * TOK_SEQ, DOUT), layer_input_gradient.reshape(seq_count * TOK_SEQ, D), grad_in, grad_out)
```

```python
import functools

import jax
import jax.numpy as jnp
from jax import lax
from jax.experimental import pallas as pl
from jax.experimental.pallas import tpu as pltpu
from jax.sharding import PartitionSpec as P

R = 64
LANES = 128
adapter_scale = 2.0
f32 = jnp.float32
bf16 = jnp.bfloat16


def grid_of(n):
    chips = n // 2
    inner = 1
    while 4 * inner * inner <= chips:
        inner *= 2
    if chips % inner:
        inner = 1
    return chips // inner, inner


def dot(a, b, ca, cb):
    return lax.dot_general(a, b, (((ca,), (cb,)), ((), ())), preferred_element_type=f32)


def step_kernel(
    n, kr, ob, wide, small,
    keys, x, g, w, a, b,
    mixed, dx, gin, gout,
    wbuf, asend, abuf, bsend, bbuf, psend, pback, osend, gcat, lowf, frozen, total,
    wz_s, wy_s, wc_s, w_r, a_s, a_r, b_s, b_r, p_s, p_r, o_s, o_r,
):
    Z, Y = grid_of(n)
    me = lax.axis_index("dp")
    z, y, c = me // (2 * Y), (me // 2) % Y, me % 2
    rows = g.shape[0]
    half = rows // 2

    def at(zz, yy, cc):
        return (zz * Y + yy) * 2 + cc

    partner = at(z, y, 1 - c)

    def remote(src, dst, ss, rs, peer):
        return pltpu.make_async_remote_copy(
            src_ref=src, dst_ref=dst, send_sem=ss, recv_sem=rs,
            device_id={"dp": peer}, device_id_type=pl.DeviceIdType.MESH,
        )

    def peer_of(k):
        return lax.rem(me + k, n)

    def x_block(e):
        if wide:
            return x[:, pl.ds(pl.multiple_of(e * kr, kr), kr)]
        return x[e]

    barrier = pltpu.get_barrier_semaphore()

    def greet(k, carry):
        pl.semaphore_signal(
            barrier, inc=1, device_id={"dp": peer_of(k)}, device_id_type=pl.DeviceIdType.MESH
        )
        return carry

    lax.fori_loop(1, n, greet, 0)
    wbuf[me] = w[...]
    pl.semaphore_wait(barrier, n - 1)

    def w_copy(e, ss, peer):
        return remote(wbuf.at[e], wbuf.at[e], ss, w_r.at[e], peer)

    def w_right(zp):
        return w_copy(at(zp, y, c), wz_s.at[0, zp], at(z + 1, y, c))

    def w_left(zp):
        return w_copy(at(zp, y, c), wz_s.at[1, zp], at(z - 1, y, c))

    def w_side(zp, j):
        return w_copy(at(zp, y, c), wy_s.at[zp, j - 1], at(z, lax.rem(y + j, Y), c))

    def w_core(zp, yp):
        return w_copy(at(zp, yp, c), wc_s.at[zp * Y + yp], partner)

    def w_arrived(e):
        w_copy(e, wc_s.at[0], partner).wait_recv()

    def w_spread(zp):
        for j in range(1, Y):
            w_side(zp, j).start()
        w_core(zp, y).start()

    @pl.when(z < Z - 1)
    def _():
        w_right(z).start()

    @pl.when(z > 0)
    def _():
        w_left(z).start()

    w_spread(z)

    def w_hop(d):
        @pl.when(z - d >= 0)
        def _():
            w_arrived(at(z - d, y, c))

            @pl.when(z < Z - 1)
            def _():
                w_right(z - d).start()

            w_spread(z - d)

        @pl.when(z + d < Z)
        def _():
            w_arrived(at(z + d, y, c))

            @pl.when(z > 0)
            def _():
                w_left(z + d).start()

            w_spread(z + d)

    pick_step = min(2048, a.shape[1])

    def named(e, off, size):
        name = lax.broadcasted_iota(jnp.int32, (size, LANES), 0) + off
        return jnp.where(name == keys[pl.ds(e, 1), :], 1.0, 0.0).astype(bf16)

    def pick(e):
        if pick_step == a.shape[1]:
            sel = named(e, 0, pick_step)
            return [dot(r[...], sel, 1, 0).astype(bf16) for r in ((b, a) if small else (a,))]
        total[:, :LANES] = jnp.zeros((kr, LANES), f32)

        def block(j, carry):
            off = pl.multiple_of(j * pick_step, pick_step)
            total[:, :LANES] += dot(a[:, pl.ds(off, pick_step)], named(e, off, pick_step), 1, 0)
            return carry

        lax.fori_loop(0, a.shape[1] // pick_step, block, 0)
        return [total[:, :LANES].astype(bf16)]

    def a_copy(e, slot):
        return remote(asend.at[e], abuf.at[slot], a_s.at[e], a_r.at[slot], e)

    def b_copy(e, slot):
        return remote(bsend.at[e], bbuf.at[slot], b_s.at[e], b_r.at[slot], e)

    def send_a(k, carry):
        e = peer_of(k)
        picked = pick(e)
        if small:
            bsend[e] = picked[0]
            b_copy(e, me).start()
        asend[e] = picked[-1]
        a_copy(e, me).start()
        return carry

    cut = n // 2
    lax.fori_loop(1, cut, send_a, 0)
    w_hop(1)
    lax.fori_loop(cut, n, send_a, 0)
    picked = pick(me)
    if small:
        bbuf[me] = picked[0]
    abuf[me] = picked[-1]

    row = lax.broadcasted_iota(jnp.int32, (rows, LANES), 0)
    col = lax.broadcasted_iota(jnp.int32, (rows, LANES), 1)
    own = (row < half) == (col < R)

    def wait_b(k, carry):
        e = peer_of(k)
        b_copy(e, e).wait()
        return carry

    if small:
        lax.fori_loop(1, n, wait_b, 0)
        up = bbuf[...].reshape(n * ob, LANES)
    else:
        up = b[...]
    width = g.shape[1]
    low_grad = jnp.where(own, adapter_scale * dot(g[...], up, 1, 0), 0.0).astype(bf16)
    gcat[:, :width] = g[...]
    gcat[:, width:] = low_grad

    def term_in(e):
        return dot(x_block(e), gcat[:, width:], 0, 0).astype(bf16)

    def p_copy(e, slot):
        return remote(psend.at[e], pback.at[slot, pl.ds(0, kr)], p_s.at[e], p_r.at[slot], e)

    def send_p(k, carry):
        e = peer_of(k)
        psend[e] = term_in(e)
        p_copy(e, me).start()
        return carry

    if Z > 2:
        w_hop(2)
    lax.fori_loop(1, cut, send_p, 0)
    for d in range(3, Z):
        w_hop(d)
    lax.fori_loop(cut, n, send_p, 0)
    pback[me, :kr] = term_in(me)

    for j in range(1, Y):
        ys = lax.rem(y + j, Y)
        for dz in range(Z):
            zp = lax.rem(z + dz, Z)
            w_arrived(at(zp, ys, c))
            w_core(zp, ys).start()

    lowf[...] = dot(x_block(me), abuf[me], 1, 0)

    def low_step(k, carry):
        e = peer_of(k)
        a_copy(e, e).wait()
        lowf[...] += dot(x_block(e), abuf[e], 1, 0)
        return carry

    lax.fori_loop(1, n, low_step, 0)
    low = jnp.where(own, lowf[...], 0.0).astype(bf16)
    term_out = (adapter_scale * dot(g[...], low, 0, 0)).astype(bf16)

    def o_copy(e, slot):
        src = osend.at[pl.ds(pl.multiple_of(e * ob, ob), ob)]
        return remote(src, pback.at[slot, pl.ds(kr, ob)], o_s.at[e], o_r.at[slot], e)

    def send_o(k, carry):
        e = peer_of(k)
        o_copy(e, me).start()
        return carry

    if small:
        osend[...] = term_out
        lax.fori_loop(1, n, send_o, 0)
        pback[me, kr:] = osend[pl.ds(pl.multiple_of(me * ob, ob), ob), :]
    else:
        gout[...] = term_out
    frozen[...] = adapter_scale * dot(low, up, 1, 1)

    for zp in range(Z):
        for yp in range(Y):
            w_arrived(at(zp, yp, 1 - c))

    def base_step(k, carry):
        e = peer_of(k)
        frozen[...] += dot(x_block(e), wbuf[e], 1, 0)
        both = jnp.concatenate([wbuf[e], abuf[e]], axis=1)
        value = dot(gcat[...], both, 1, 1).astype(bf16)
        if wide:
            dx[:, pl.ds(pl.multiple_of(e * kr, kr), kr)] = value
        else:
            dx[e] = value
        return carry

    lax.fori_loop(0, n, base_step, 0)
    mixed[...] = frozen[...].astype(bf16)

    step = min(512, total.shape[1])
    blocks = total.shape[1] // step
    total[...] = jnp.zeros_like(total)

    def own_sum(e):
        def block(j, carry):
            off = pl.multiple_of(j * step, step)
            total[:, pl.ds(off, step)] += dot(pback[e], named(e, off, step), 1, 1)
            return carry

        lax.fori_loop(0, blocks, block, 0)

    own_sum(me)

    def sum_step(k, carry):
        e = peer_of(k)
        p_copy(e, e).wait()
        if small:
            o_copy(e, e).wait()
        own_sum(e)
        return carry

    lax.fori_loop(1, n, sum_step, 0)
    gin[...] = total[:kr, :].astype(bf16)
    if small:
        gout[...] = total[kr:, :].astype(bf16)

    for zp in range(Z):
        @pl.when((zp <= z) & (z < Z - 1))
        def _(zp=zp):
            w_right(zp).wait_send()

        @pl.when((zp >= z) & (z > 0))
        def _(zp=zp):
            w_left(zp).wait_send()

        for j in range(1, Y):
            w_side(zp, j).wait_send()
        for yp in range(Y):
            w_core(zp, yp).wait_send()


def body(tokens, out_grad, base_weight, adapter_in, adapter_out, tenant_ids):
    n = lax.axis_size("dp")
    rows, depth = tokens.shape
    width = out_grad.shape[1]
    kr = adapter_in.shape[0]
    orows = adapter_out.shape[0]
    columns = adapter_in.shape[1]
    wide = kr % LANES == 0
    small = orows % 16 == 0
    ob = orows if small else 16
    slots = tenant_ids.shape[0] // n
    assert slots * R == LANES
    Z, Y = grid_of(n)

    keys = (tenant_ids[:, None] * R + jnp.arange(R, dtype=jnp.int32)[None, :]).reshape(n, LANES)
    if wide:
        x, dx_shape = tokens, (rows, depth)
    else:
        x = tokens.reshape(rows, n, kr).transpose(1, 0, 2)
        dx_shape = (n, rows, kr)
    if small:
        b, gout_shape = adapter_out, (orows, columns)
    else:
        table = adapter_out.reshape(orows, columns // R, R)
        sent = jnp.take(table, tenant_ids, axis=1).reshape(orows, n, LANES).transpose(1, 0, 2)
        b = lax.all_to_all(sent, "dp", split_axis=0, concat_axis=0, tiled=True).reshape(width, LANES)
        gout_shape = (width, LANES)
    vmem = pl.BlockSpec(memory_space=pltpu.VMEM)
    dma = pltpu.SemaphoreType.DMA
    trows = kr + ob if small else kr
    mixed, dx, grad_in, out_part = pl.pallas_call(
        functools.partial(step_kernel, n, kr, ob, wide, small),
        out_shape=(
            jax.ShapeDtypeStruct((rows, width), bf16),
            jax.ShapeDtypeStruct(dx_shape, bf16),
            jax.ShapeDtypeStruct((kr, columns), bf16),
            jax.ShapeDtypeStruct(gout_shape, bf16),
        ),
        in_specs=[vmem] * 6,
        out_specs=[vmem] * 4,
        scratch_shapes=[
            pltpu.VMEM((n, kr, width), bf16),
            pltpu.VMEM((n, kr, LANES), bf16),
            pltpu.VMEM((n, kr, LANES), bf16),
            pltpu.VMEM((n, ob, LANES), bf16),
            pltpu.VMEM((n, ob, LANES), bf16),
            pltpu.VMEM((n, kr, LANES), bf16),
            pltpu.VMEM((n, trows, LANES), bf16),
            pltpu.VMEM((n * ob, LANES), bf16),
            pltpu.VMEM((rows, width + LANES), bf16),
            pltpu.VMEM((rows, LANES), f32),
            pltpu.VMEM((rows, width), f32),
            pltpu.VMEM((trows, columns), f32),
            dma((2, Z)), dma((Z, max(Y - 1, 1))), dma((Z * Y,)), dma((n,)),
            dma((n,)), dma((n,)), dma((n,)), dma((n,)),
            dma((n,)), dma((n,)), dma((n,)), dma((n,)),
        ],
        compiler_params=pltpu.CompilerParams(
            collective_id=0, has_side_effects=True, vmem_limit_bytes=58 * 1024 * 1024
        ),
        cost_estimate=pl.CostEstimate(
            flops=8 * rows * depth * (width + LANES), bytes_accessed=8 * rows * depth, transcendentals=0
        ),
    )(keys, x, out_grad, base_weight, adapter_in, b)
    if not wide:
        dx = dx.transpose(1, 0, 2).reshape(rows, depth)
    if small:
        grad_out = out_part
    else:
        got = lax.all_to_all(
            out_part.reshape(n, orows, LANES), "dp", split_axis=0, concat_axis=0, tiled=True
        )
        moved = got.reshape(n, orows, slots, R).transpose(0, 2, 1, 3).reshape(n * slots, orows, R)
        summed = jax.ops.segment_sum(
            moved.astype(f32), tenant_ids, num_segments=columns // R
        )
        grad_out = summed.transpose(1, 0, 2).reshape(orows, columns).astype(bf16)
    return mixed, dx, grad_in, grad_out


def solution(mesh):
    in_specs = (
        P(("groups", "dp"), None),
        P(("groups", "dp"), None),
        P("dp", None),
        P("dp", "groups"),
        P("dp", "groups"),
        P("groups"),
    )
    out_specs = (
        P(("groups", "dp"), None),
        P(("groups", "dp"), None),
        P("dp", "groups"),
        P("dp", "groups"),
    )
    return jax.shard_map(body, mesh=mesh, in_specs=in_specs, out_specs=out_specs, check_vma=False)
```

```python
import functools

import jax
import jax.numpy as jnp
from jax import lax
from jax.experimental import pallas as pl
from jax.experimental.pallas import tpu as pltpu
from jax.sharding import PartitionSpec as P

R = 64
LANES = 128
adapter_scale = 2.0
f32 = jnp.float32
bf16 = jnp.bfloat16


def grid_of(n):
    chips = n // 2
    inner = 1
    while 4 * inner * inner <= chips:
        inner *= 2
    if chips % inner:
        inner = 1
    return chips // inner, inner


def dot(a, b, ca, cb):
    return lax.dot_general(a, b, (((ca,), (cb,)), ((), ())), preferred_element_type=f32)


def step_kernel(
    n, kr, ob, wide, small,
    keys, x, g, w, a, b,
    mixed, dx, gin, gout,
    wbuf, asend, abuf, bsend, bbuf, psend, pback, osend, gcat, lowf, frozen, total,
    wz_s, wy_s, wc_s, w_r, a_s, a_r, b_s, b_r, p_s, p_r, o_s, o_r,
):
    Z, Y = grid_of(n)
    me = lax.axis_index("dp")
    z, y, c = me // (2 * Y), (me // 2) % Y, me % 2
    rows = g.shape[0]
    half = rows // 2

    def at(zz, yy, cc):
        return (zz * Y + yy) * 2 + cc

    partner = at(z, y, 1 - c)

    def remote(src, dst, ss, rs, peer):
        return pltpu.make_async_remote_copy(
            src_ref=src, dst_ref=dst, send_sem=ss, recv_sem=rs,
            device_id={"dp": peer}, device_id_type=pl.DeviceIdType.MESH,
        )

    def peer_of(k):
        p = (k + n - 1) % n
        q, r = p // (2 * Y), p % (2 * Y)
        far = (q + 1) // 2
        dz = Z // 2 + far - 2 * far * (q % 2)
        r = (r + 1) % (2 * Y)
        return at((z + dz + Z) % Z, (y + r // 2) % Y, (c + r % 2) % 2)

    def x_block(e):
        if wide:
            return x[:, pl.ds(pl.multiple_of(e * kr, kr), kr)]
        return x[e]

    barrier = pltpu.get_barrier_semaphore()

    def greet(k, carry):
        pl.semaphore_signal(
            barrier, inc=1, device_id={"dp": peer_of(k)}, device_id_type=pl.DeviceIdType.MESH
        )
        return carry

    lax.fori_loop(1, n, greet, 0)
    wbuf[me] = w[...]
    pl.semaphore_wait(barrier, n - 1)

    def w_copy(e, ss, peer):
        return remote(wbuf.at[e], wbuf.at[e], ss, w_r.at[e], peer)

    def w_right(zp):
        return w_copy(at(zp, y, c), wz_s.at[0, zp], at(z + 1, y, c))

    def w_left(zp):
        return w_copy(at(zp, y, c), wz_s.at[1, zp], at(z - 1, y, c))

    def w_side(zp, j):
        return w_copy(at(zp, y, c), wy_s.at[zp, j - 1], at(z, lax.rem(y + j, Y), c))

    def w_core(zp, yp):
        return w_copy(at(zp, yp, c), wc_s.at[zp * Y + yp], partner)

    def w_arrived(e):
        w_copy(e, wc_s.at[0], partner).wait_recv()

    def w_spread(zp):
        for j in range(1, Y):
            w_side(zp, j).start()
        w_core(zp, y).start()

    @pl.when(z < Z - 1)
    def _():
        w_right(z).start()

    @pl.when(z > 0)
    def _():
        w_left(z).start()

    w_spread(z)

    def w_hop(d):
        @pl.when(z - d >= 0)
        def _():
            w_arrived(at(z - d, y, c))

            @pl.when(z < Z - 1)
            def _():
                w_right(z - d).start()

            w_spread(z - d)

        @pl.when(z + d < Z)
        def _():
            w_arrived(at(z + d, y, c))

            @pl.when(z > 0)
            def _():
                w_left(z + d).start()

            w_spread(z + d)

    pick_step = min(2048, a.shape[1])

    def named(e, off, size):
        name = lax.broadcasted_iota(jnp.int32, (size, LANES), 0) + off
        return jnp.where(name == keys[pl.ds(e, 1), :], 1.0, 0.0).astype(bf16)

    def pick(e):
        if pick_step == a.shape[1]:
            sel = named(e, 0, pick_step)
            return [dot(r[...], sel, 1, 0).astype(bf16) for r in ((b, a) if small else (a,))]
        total[:, :LANES] = jnp.zeros((kr, LANES), f32)

        def block(j, carry):
            off = pl.multiple_of(j * pick_step, pick_step)
            total[:, :LANES] += dot(a[:, pl.ds(off, pick_step)], named(e, off, pick_step), 1, 0)
            return carry

        lax.fori_loop(0, a.shape[1] // pick_step, block, 0)
        return [total[:, :LANES].astype(bf16)]

    def a_copy(e, slot):
        return remote(asend.at[e], abuf.at[slot], a_s.at[e], a_r.at[slot], e)

    def b_copy(e, slot):
        return remote(bsend.at[e], bbuf.at[slot], b_s.at[e], b_r.at[slot], e)

    def send_a(k, carry):
        e = peer_of(k)
        picked = pick(e)
        if small:
            bsend[e] = picked[0]
            b_copy(e, me).start()
        asend[e] = picked[-1]
        a_copy(e, me).start()
        return carry

    hops = max(Z - 1, 1)
    cuts = [1 + (n - 1) * d // hops for d in range(hops + 1)]
    for d in range(1, hops):
        lax.fori_loop(cuts[d - 1], cuts[d], send_a, 0)
        w_hop(d)
    lax.fori_loop(cuts[hops - 1], n, send_a, 0)
    picked = pick(me)
    if small:
        bbuf[me] = picked[0]
    abuf[me] = picked[-1]

    row = lax.broadcasted_iota(jnp.int32, (rows, LANES), 0)
    col = lax.broadcasted_iota(jnp.int32, (rows, LANES), 1)
    own = (row < half) == (col < R)

    def wait_b(k, carry):
        e = peer_of(k)
        b_copy(e, e).wait()
        return carry

    if small:
        lax.fori_loop(1, n, wait_b, 0)
        up = bbuf[...].reshape(n * ob, LANES)
    else:
        up = b[...]
    width = g.shape[1]
    low_grad = jnp.where(own, adapter_scale * dot(g[...], up, 1, 0), 0.0).astype(bf16)
    gcat[:, :width] = g[...]
    gcat[:, width:] = low_grad

    def term_in(e):
        return dot(x_block(e), gcat[:, width:], 0, 0).astype(bf16)

    def p_copy(e, slot):
        return remote(psend.at[e], pback.at[slot, pl.ds(0, kr)], p_s.at[e], p_r.at[slot], e)

    def send_p(k, carry):
        e = peer_of(k)
        psend[e] = term_in(e)
        p_copy(e, me).start()
        return carry

    w_hop(Z - 1)
    lax.fori_loop(1, n // 2, send_p, 0)
    for j in range(1, Y):
        ys = lax.rem(y + j, Y)
        for dz in range(Z):
            zp = lax.rem(z + dz, Z)
            w_arrived(at(zp, ys, c))
            w_core(zp, ys).start()

    lax.fori_loop(n // 2, n, send_p, 0)
    pback[me, :kr] = term_in(me)
    lowf[...] = dot(x_block(me), abuf[me], 1, 0)

    def low_step(k, carry):
        e = peer_of(k)
        a_copy(e, e).wait()
        lowf[...] += dot(x_block(e), abuf[e], 1, 0)
        return carry

    lax.fori_loop(1, n, low_step, 0)
    low = jnp.where(own, lowf[...], 0.0).astype(bf16)
    term_out = (adapter_scale * dot(g[...], low, 0, 0)).astype(bf16)

    def o_copy(e, slot):
        src = osend.at[pl.ds(pl.multiple_of(e * ob, ob), ob)]
        return remote(src, pback.at[slot, pl.ds(kr, ob)], o_s.at[e], o_r.at[slot], e)

    def send_o(k, carry):
        e = peer_of(k)
        o_copy(e, me).start()
        return carry

    if small:
        osend[...] = term_out
        lax.fori_loop(1, n, send_o, 0)
        pback[me, kr:] = osend[pl.ds(pl.multiple_of(me * ob, ob), ob), :]
    else:
        gout[...] = term_out
    frozen[...] = adapter_scale * dot(low, up, 1, 1)

    for zp in range(Z):
        for yp in range(Y):
            w_arrived(at(zp, yp, 1 - c))

    def base_step(k, carry):
        e = peer_of(k)
        frozen[...] += dot(x_block(e), wbuf[e], 1, 0)
        both = jnp.concatenate([wbuf[e], abuf[e]], axis=1)
        value = dot(gcat[...], both, 1, 1).astype(bf16)
        if wide:
            dx[:, pl.ds(pl.multiple_of(e * kr, kr), kr)] = value
        else:
            dx[e] = value
        return carry

    lax.fori_loop(0, n, base_step, 0)
    mixed[...] = frozen[...].astype(bf16)

    step = min(512, total.shape[1])
    blocks = total.shape[1] // step
    total[...] = jnp.zeros_like(total)

    group = min(4, n)

    def sum_step(i, carry):
        peers = [peer_of(i * group + k) for k in range(group)]

        def arrived(e):
            p_copy(e, e).wait()
            if small:
                o_copy(e, e).wait()

        for k, e in enumerate(peers):
            if k == 0:
                pl.when(i > 0)(functools.partial(arrived, e))
            else:
                arrived(e)
        terms = jnp.concatenate([pback[e] for e in peers], axis=1)

        def block(j, carry):
            off = pl.multiple_of(j * step, step)
            sel = jnp.concatenate([named(e, off, step) for e in peers], axis=1)
            total[:, pl.ds(off, step)] += dot(terms, sel, 1, 1)
            return carry

        return lax.fori_loop(0, blocks, block, carry)

    lax.fori_loop(0, n // group, sum_step, 0)
    gin[...] = total[:kr, :].astype(bf16)
    if small:
        gout[...] = total[kr:, :].astype(bf16)

    for zp in range(Z):
        @pl.when((zp <= z) & (z < Z - 1))
        def _(zp=zp):
            w_right(zp).wait_send()

        @pl.when((zp >= z) & (z > 0))
        def _(zp=zp):
            w_left(zp).wait_send()

        for j in range(1, Y):
            w_side(zp, j).wait_send()
        for yp in range(Y):
            w_core(zp, yp).wait_send()


def body(tokens, out_grad, base_weight, adapter_in, adapter_out, tenant_ids):
    n = lax.axis_size("dp")
    rows, depth = tokens.shape
    width = out_grad.shape[1]
    kr = adapter_in.shape[0]
    orows = adapter_out.shape[0]
    columns = adapter_in.shape[1]
    wide = kr % LANES == 0
    small = orows % 16 == 0
    ob = orows if small else 16
    slots = tenant_ids.shape[0] // n
    assert slots * R == LANES
    Z, Y = grid_of(n)

    keys = (tenant_ids[:, None] * R + jnp.arange(R, dtype=jnp.int32)[None, :]).reshape(n, LANES)
    if wide:
        x, dx_shape = tokens, (rows, depth)
    else:
        x = tokens.reshape(rows, n, kr).transpose(1, 0, 2)
        dx_shape = (n, rows, kr)
    if small:
        b, gout_shape = adapter_out, (orows, columns)
    else:
        table = adapter_out.reshape(orows, columns // R, R)
        sent = jnp.take(table, tenant_ids, axis=1).reshape(orows, n, LANES).transpose(1, 0, 2)
        b = lax.all_to_all(sent, "dp", split_axis=0, concat_axis=0, tiled=True).reshape(width, LANES)
        gout_shape = (width, LANES)
    vmem = pl.BlockSpec(memory_space=pltpu.VMEM)
    dma = pltpu.SemaphoreType.DMA
    trows = kr + ob if small else kr
    mixed, dx, grad_in, out_part = pl.pallas_call(
        functools.partial(step_kernel, n, kr, ob, wide, small),
        out_shape=(
            jax.ShapeDtypeStruct((rows, width), bf16),
            jax.ShapeDtypeStruct(dx_shape, bf16),
            jax.ShapeDtypeStruct((kr, columns), bf16),
            jax.ShapeDtypeStruct(gout_shape, bf16),
        ),
        in_specs=[vmem] * 6,
        out_specs=[vmem] * 4,
        scratch_shapes=[
            pltpu.VMEM((n, kr, width), bf16),
            pltpu.VMEM((n, kr, LANES), bf16),
            pltpu.VMEM((n, kr, LANES), bf16),
            pltpu.VMEM((n, ob, LANES), bf16),
            pltpu.VMEM((n, ob, LANES), bf16),
            pltpu.VMEM((n, kr, LANES), bf16),
            pltpu.VMEM((n, trows, LANES), bf16),
            pltpu.VMEM((n * ob, LANES), bf16),
            pltpu.VMEM((rows, width + LANES), bf16),
            pltpu.VMEM((rows, LANES), f32),
            pltpu.VMEM((rows, width), f32),
            pltpu.VMEM((trows, columns), f32),
            dma((2, Z)), dma((Z, max(Y - 1, 1))), dma((Z * Y,)), dma((n,)),
            dma((n,)), dma((n,)), dma((n,)), dma((n,)),
            dma((n,)), dma((n,)), dma((n,)), dma((n,)),
        ],
        compiler_params=pltpu.CompilerParams(
            collective_id=0, has_side_effects=True, vmem_limit_bytes=58 * 1024 * 1024
        ),
        cost_estimate=pl.CostEstimate(
            flops=8 * rows * depth * (width + LANES), bytes_accessed=8 * rows * depth, transcendentals=0
        ),
    )(keys, x, out_grad, base_weight, adapter_in, b)
    if not wide:
        dx = dx.transpose(1, 0, 2).reshape(rows, depth)
    if small:
        grad_out = out_part
    else:
        got = lax.all_to_all(
            out_part.reshape(n, orows, LANES), "dp", split_axis=0, concat_axis=0, tiled=True
        )
        moved = got.reshape(n, orows, slots, R).transpose(0, 2, 1, 3).reshape(n * slots, orows, R)
        summed = jax.ops.segment_sum(
            moved.astype(f32), tenant_ids, num_segments=columns // R
        )
        grad_out = summed.transpose(1, 0, 2).reshape(orows, columns).astype(bf16)
    return mixed, dx, grad_in, grad_out


def solution(mesh):
    in_specs = (
        P(("groups", "dp"), None),
        P(("groups", "dp"), None),
        P("dp", None),
        P("dp", "groups"),
        P("dp", "groups"),
        P("groups"),
    )
    out_specs = (
        P(("groups", "dp"), None),
        P(("groups", "dp"), None),
        P("dp", "groups"),
        P("dp", "groups"),
    )
    return jax.shard_map(body, mesh=mesh, in_specs=in_specs, out_specs=out_specs, check_vma=False)
```
